256 devices in a mesh: lat: 8 (over x, core), lon: 16 (over z, y_lo), dp: 2 (over y_hi).
Axes of the slice: x: 4, y: 4 (y_hi: 2, y_lo: 2; y = y_hi * 2 + y_lo), z: 8, core: 2. Of those that a mesh axis runs over, the one named last changes fastest.
Arguments:
- node_latent: bfloat16 [2, 8, 16, 256, 512], P('dp', 'lat', 'lon'), may hold values from -6 to 6
- edge_latent: bfloat16 [2, 8, 16, 384, 512], P('dp', 'lat', 'lon'), may hold values from -6 to 6
- senders: int32 [8, 16, 384], P('lat', 'lon'), may hold values from 0 to 1791, as said below
- receivers: int32 [8, 16, 384], P('lat', 'lon'), may hold values from 0 to 255
- edge_live: int32 [8, 16, 384], P('lat', 'lon'), may hold values 0 or 1
- halo_list: int32 [8, 16, 128], P('lat', 'lon'), may hold values from 0 to 255
- coarse_list: int32 [8, 16, 8], P('lat', 'lon'), may hold values from 0 to 255
- edge_in_w: bfloat16 [1536, 512], replicated, may hold values from -0.15625 to 0.15625
- edge_out_w: bfloat16 [512, 512], replicated, may hold values from -0.25 to 0.25
- node_in_w: bfloat16 [1024, 512], replicated, may hold values from -0.1875 to 0.1875
- node_out_w: bfloat16 [512, 512], replicated, may hold values from -0.25 to 0.25
- edge_gain: float32 [512], replicated, may hold values from 0.25 to 1.75
- node_gain: float32 [512], replicated, may hold values from 0.25 to 1.75
- node_cot: bfloat16 [2, 8, 16, 256, 512], P('dp', 'lat', 'lon'), may hold values from -6 to 6
- edge_cot: bfloat16 [2, 8, 16, 384, 512], P('dp', 'lat', 'lon'), may hold values from -6 to 6
Outputs:
- new_nodes: bfloat16 [2, 8, 16, 256, 512], P('dp', 'lat', 'lon')
- new_edges: bfloat16 [2, 8, 16, 384, 512], P('dp', 'lat', 'lon')
- node_grad: bfloat16 [2, 8, 16, 256, 512], P('dp', 'lat', 'lon')
- edge_grad: bfloat16 [2, 8, 16, 384, 512], P('dp', 'lat', 'lon')
- weight_grad: float32 [1835008], P(('lat', 'lon', 'dp'))
- gain_grad: float32 [2, 512], replicated
The draws below stay inside these ranges and needn't reach their ends.
Inputs may be any that keep to these rules, and one draw needn't show every extreme that they name: `senders`: rows below 256 are own nodes, the next 512 rows the lower, upper, west and east rim lists, the rest the coarse rows.
All inputs are finite; a program needn't handle non-finite values. No bound on the sum of `edge_live` on one device may be relied on, other than what follows from the above.
Results may differ from the reference program's by a relative error of at most 0.015.
Values may be sent and summed in bfloat16 or wider, within the bound.
No kernel may reach another device: no remote copies, remote signals or barrier semaphores. Data moves between devices by JAX's collectives and lax.ppermute only.
A program may use at most 128 MiB of HBM per device.

```python
import math
import jax
import jax.numpy as jnp
from jax import lax

D = 512
H = 512
NODE_DEV = 256
EDGE_DEV = 384
HALO = 128
COARSE_DEV = 8
SAMPLES = 2
BANDS = 8
SECTORS = 16
TABLE = 1792
EDGES = 98304


def draw_senders(key, part):
    key = jax.random.fold_in(key, 11)
    keys = jax.random.split(key, 5)
    shape = (BANDS, SECTORS, EDGE_DEV)
    kind = jax.random.randint(keys[0], shape, 0, 10)
    own_rows = jax.random.randint(keys[1], shape, 0, NODE_DEV)
    rim_rows = jax.random.randint(keys[2], shape, NODE_DEV, NODE_DEV + 4 * HALO)
    coarse_rows = jax.random.randint(keys[3], shape, NODE_DEV + 4 * HALO, TABLE)
    picked = jnp.where(kind < 5, own_rows, jnp.where(kind < 8, rim_rows, coarse_rows))
    blocks = BANDS * SECTORS
    flat_index = (jnp.arange(BANDS, dtype=jnp.int32)[:, None] * SECTORS + jnp.arange(SECTORS, dtype=jnp.int32)[None, :])[:, :, None]
    opposite = (flat_index + blocks // 2) % blocks
    within = jax.random.randint(keys[4], shape, 0, COARSE_DEV)
    far_rows = NODE_DEV + 4 * HALO + opposite * COARSE_DEV + within
    position = lax_iota(shape)
    picked = jnp.where((position >= 2) & (position < 2 + EDGE_DEV // 4), far_rows, picked)
    picked = jnp.where(position == 0, TABLE - 1, jnp.where(position == 1, 0, picked))
    return picked.astype(jnp.int32)


def lax_iota(shape):
    return jnp.broadcast_to(jnp.arange(shape[2], dtype=jnp.int32), shape)


def plant(result, rng, low, top_value):
    longest = result.shape.index(max(result.shape))
    spots = []
    for shift in (0, 1):
        where = [jax.random.randint(jax.random.fold_in(rng, axis), (), 0, length) for axis, length in enumerate(result.shape)]
        where[longest] = (where[longest] + shift) % result.shape[longest]
        spots.append(tuple(where))
    return result.at[spots[0]].set(low).at[spots[1]].set(top_value)


def block_levels(rng, extent, pieces, smallest, top_value):
    def one(dim, blocks):
        steps = jax.random.uniform(jax.random.fold_in(jax.random.fold_in(rng, 6), dim), (blocks,), jnp.float32, smallest / len(pieces), top_value / len(pieces))
        return jnp.repeat(jnp.exp(steps), extent[dim] // blocks).reshape((-1,) + (1,) * (len(extent) - dim - 1))

    level = one(*pieces[0])
    for cut in pieces[1:]:
        level = level * one(*cut)
    return level


def bell_draw(rng, extent, scale, most, cuts=(), kind=jnp.bfloat16):
    entries = scale * jax.random.normal(rng, extent, jnp.float32)
    if cuts:
        entries = entries * block_levels(rng, extent, cuts, -0.22, 0.18)
    return jnp.clip(entries, -most, most).astype(kind)


def setup_inputs(seed: int = 0) -> dict:
    splits = jax.random.split(jax.random.key(seed), 16)
    return {
        "node_latent": bell_draw(splits[0], (SAMPLES, BANDS, SECTORS, NODE_DEV, D), 1.0, 6.0, ((0, 2), (1, 8), (2, 16))),
        "edge_latent": bell_draw(splits[1], (SAMPLES, BANDS, SECTORS, EDGE_DEV, D), 1.0, 6.0, ((0, 2), (1, 8), (2, 16))),
        "senders": draw_senders(jax.random.fold_in(splits[15], 71), 0),
        "receivers": plant(jax.random.randint(splits[3], (BANDS, SECTORS, EDGE_DEV), 0, NODE_DEV), jax.random.fold_in(splits[3], 1), 0, NODE_DEV - 1).astype(jnp.int32),
        "edge_live": plant((jax.random.randint(splits[4], (BANDS, SECTORS, EDGE_DEV), 0, 4) < 3).astype(jnp.int32), jax.random.fold_in(splits[4], 1), 0, 1),
        "halo_list": plant(jax.random.randint(splits[5], (BANDS, SECTORS, HALO), 0, NODE_DEV), jax.random.fold_in(splits[5], 1), 0, NODE_DEV - 1).astype(jnp.int32),
        "coarse_list": plant(jax.random.randint(splits[6], (BANDS, SECTORS, COARSE_DEV), 0, NODE_DEV), jax.random.fold_in(splits[6], 1), 0, NODE_DEV - 1).astype(jnp.int32),
        "edge_in_w": bell_draw(splits[7], (3 * D, H), (3 * D) ** -0.5, 0.15625),
        "edge_out_w": bell_draw(splits[8], (H, D), H ** -0.5, 0.25),
        "node_in_w": bell_draw(splits[9], (2 * D, H), (2 * D) ** -0.5, 0.1875),
        "node_out_w": bell_draw(splits[10], (H, D), H ** -0.5, 0.25),
        "edge_gain": jnp.clip(1.0 + 0.15 * jax.random.normal(splits[11], (D,), jnp.float32), 0.25, 1.75),
        "node_gain": jnp.clip(1.0 + 0.15 * jax.random.normal(splits[12], (D,), jnp.float32), 0.25, 1.75),
        "node_cot": bell_draw(splits[13], (SAMPLES, BANDS, SECTORS, NODE_DEV, D), 1.0, 6.0, ((0, 2), (1, 8), (2, 16))),
        "edge_cot": bell_draw(splits[14], (SAMPLES, BANDS, SECTORS, EDGE_DEV, D), 1.0, 6.0, ((0, 2), (1, 8), (2, 16))),
    }


def layer_norm(values, gain):
    center = values - lax.optimization_barrier(jnp.mean(values, axis=-1, keepdims=True))
    spread = lax.optimization_barrier(jnp.mean(center * center, axis=-1, keepdims=True))
    return center * lax.rsqrt(spread + 1e-05) * gain

def local_layer(send, recv, live, table, own, edges, w_ein, w_eout, w_nin, w_nout, gain_e, gain_n):
    count = own.shape[0]
    from_send = jnp.take(table, send, axis=0)
    from_recv = jnp.take(own, recv, axis=0)
    joined = jnp.concatenate([from_send, from_recv, edges], axis=-1).astype(jnp.bfloat16)
    hidden = jax.nn.silu(jnp.dot(joined, w_ein.astype(jnp.bfloat16), preferred_element_type=jnp.float32)).astype(jnp.bfloat16)
    message = layer_norm(jnp.dot(hidden, w_eout.astype(jnp.bfloat16), preferred_element_type=jnp.float32), gain_e)
    new_edge = (edges + message).astype(jnp.bfloat16)
    pooled = jax.ops.segment_sum(message * live[:, None].astype(jnp.float32), recv, num_segments=count)
    node_input = jnp.concatenate([own, pooled], axis=-1).astype(jnp.bfloat16)
    node_hidden = jax.nn.silu(jnp.dot(node_input, w_nin.astype(jnp.bfloat16), preferred_element_type=jnp.float32)).astype(jnp.bfloat16)
    update = layer_norm(jnp.dot(node_hidden, w_nout.astype(jnp.bfloat16), preferred_element_type=jnp.float32), gain_n)
    new_node = (own + update).astype(jnp.bfloat16)
    return (new_node, new_edge)

def reference(node_latent, edge_latent, senders, receivers, edge_live, halo_list, coarse_list, edge_in_w, edge_out_w, node_in_w, node_out_w, edge_gain, node_gain, node_cot, edge_cot):
    blocks = SAMPLES * BANDS * SECTORS

    def forward(node32, edge32, w_a, w_b, w_c, w_d, gain_e, gain_n):

        def one_block(index):
            sample = index // (BANDS * SECTORS)
            band = index // SECTORS % BANDS
            sector = index % SECTORS

            def outgoing(band_at, sector_at):
                return jnp.take(node32[sample, band_at, sector_at], halo_list[band_at, sector_at], axis=0)
            lower = outgoing(jnp.maximum(band - 1, 0), sector) * (band > 0).astype(jnp.float32)
            upper = outgoing(jnp.minimum(band + 1, BANDS - 1), sector) * (band < BANDS - 1).astype(jnp.float32)
            west = outgoing(band, (sector - 1) % SECTORS)
            east = outgoing(band, (sector + 1) % SECTORS)
            coarse = jnp.take_along_axis(node32[sample], coarse_list[:, :, :, None], axis=2)
            coarse = coarse.reshape(BANDS * SECTORS * COARSE_DEV, D)
            own = node32[sample, band, sector]
            table = jnp.concatenate([own, lower, upper, west, east, coarse], axis=0)
            return local_layer(senders[band, sector], receivers[band, sector], edge_live[band, sector], table, own, edge32[sample, band, sector], w_a, w_b, w_c, w_d, gain_e, gain_n)
        fresh_nodes, fresh_edges = lax.map(jax.checkpoint(one_block), jnp.arange(blocks, dtype=jnp.int32))
        return (fresh_nodes.reshape(node_latent.shape), fresh_edges.reshape(edge_latent.shape))
    primal, pullback = jax.vjp(forward, node_latent.astype(jnp.float32), edge_latent.astype(jnp.float32), edge_in_w.astype(jnp.float32), edge_out_w.astype(jnp.float32), node_in_w.astype(jnp.float32), node_out_w.astype(jnp.float32), edge_gain, node_gain)
    grads = pullback((node_cot, edge_cot))
    factor = 1.0 / math.sqrt(EDGES)
    weight_grad = jnp.concatenate([grads[2].reshape(-1), grads[3].reshape(-1), grads[4].reshape(-1), grads[5].reshape(-1)]) * factor
    gain_grad = jnp.stack([grads[6], grads[7]]) * factor
    return (primal[0], primal[1], grads[0].astype(jnp.bfloat16), grads[1].astype(jnp.bfloat16), weight_grad, gain_grad)
```

```python
import functools

import jax
import jax.numpy as jnp
from jax import lax
from jax.sharding import PartitionSpec as P

AXES = ("lat", "lon", "dp")
F32 = jnp.float32
BF16 = jnp.bfloat16
WIDTH = 512
UNIT = 304


def shifted(block, axis, distance):
    devices = range(lax.axis_size(axis))
    route = [(i - distance, i) for i in devices if i - distance in devices]
    return lax.ppermute(block, axis, route)


def from_behind(value, axis, steps):
    count = lax.axis_size(axis)
    pairs = [(source, (source + steps) % count) for source in range(count)]
    return lax.ppermute(value, axis, pairs)


def partner_of(index, how):
    x, core, z = index >> 6, index >> 5 & 1, index >> 2 & 7
    y_lo, y_hi = index >> 1 & 1, index & 1
    kind, amount = how
    if kind == "core":
        core ^= 1
    elif kind == "x":
        x ^= amount
    elif kind == "z":
        z ^= amount
    elif kind == "y":
        y_lo ^= amount & 1
        y_hi ^= amount >> 1
    return ((x * 2 + core) * 8 + z) * 4 + y_lo * 2 + y_hi


def exchange(value, kind, amount=1):
    pairs = [(i, partner_of(i, (kind, amount))) for i in range(256)]
    return lax.ppermute(value, AXES, pairs)


def position():
    lat, lon, dp = (lax.axis_index(axis) for axis in AXES)
    return lat >> 1, lat & 1, lon >> 1, lon & 1, dp


def gather_coarse(rows):
    for kind, amount in (("y", 1), ("z", 1), ("z", 2), ("z", 4), ("x", 1), ("x", 3), ("core", 1)):
        rows = jnp.concatenate([rows, exchange(rows, kind, amount)], axis=0)
    return rows


def coarse_slot(row):
    x, core, z, y_lo, _ = position()
    owner, within = row >> 3, row & 7
    dx = (owner >> 5) ^ x
    dcore = (owner >> 4 & 1) ^ core
    dz = (owner >> 1 & 7) ^ z
    dy = (owner & 1) ^ y_lo
    high = dx >> 1
    xslot = high * 2 + ((dx & 1) ^ high)
    return ((((dcore * 4 + xslot) * 8 + dz) * 2 + dy) << 3) + within


def plus(kept, received):
    return (kept.astype(F32) + received.astype(F32)).astype(BF16)


def reduce_all(keep, send):
    x, core, z, y_lo, y_hi = position()
    total = plus(keep, exchange(send, "core"))
    a, b = total[0], total[1]
    got_a, got_b = exchange(a[2:], "x", 3), exchange(b[2:], "x", 1)
    a, b = plus(a[:2], got_a), plus(b[:2], got_b)
    got_a, got_b = exchange(a[1:], "x", 1), exchange(b[1:], "x", 3)
    a, b = plus(a[:1], got_a), plus(b[:1], got_b)
    ab = jnp.concatenate([a, b], axis=0)
    weights = ab[:, :224].reshape(8, 56, WIDTH)
    coarse = ab[:, 224:288].reshape(8, 16, WIDTH)
    gains = jnp.broadcast_to(a[:, 288:296], (8, 8, WIDTH))
    chunks = jnp.concatenate([weights, coarse, gains], axis=1)
    chunks = chunks.reshape(2, 4, 80, WIDTH)
    low = z & 3
    order = jnp.stack([low, low ^ 2, low ^ 1, low ^ 3])
    chunks = jnp.take(chunks, order, axis=1)
    kept = plus(chunks[:, :2], exchange(chunks[:, 2:], "z", 1))
    kept = plus(kept[:, :1], exchange(kept[:, 1:], "z", 2))[:, 0]
    own = lax.dynamic_index_in_dim(kept, z >> 2, 0, keepdims=False)
    other = lax.dynamic_index_in_dim(kept, 1 - (z >> 2), 0, keepdims=False)
    own = plus(own, exchange(other, "z", 4))
    weights = own[:56].reshape(2, 2, 14, WIDTH)
    coarse = own[56:72].reshape(2, 8, WIDTH)
    gains = own[72:80]
    mine = lax.dynamic_index_in_dim(weights, y_hi, 1, keepdims=False)
    theirs = lax.dynamic_index_in_dim(weights, 1 - y_hi, 1, keepdims=False)
    pack = exchange(jnp.concatenate([theirs.reshape(28, WIDTH), gains], axis=0), "y", 3)
    mine = plus(mine, pack[:28].reshape(2, 14, WIDTH))
    gains = plus(gains, pack[28:])

    def pick(array, which):
        return lax.dynamic_index_in_dim(array, which, 0, keepdims=False)

    pack = exchange(jnp.concatenate([pick(coarse, 1 - y_lo), gains, pick(mine, 1 - y_lo)], axis=0), "y", 1)
    coarse = pick(coarse, y_lo).astype(F32) + pack[:8].astype(F32)
    gains = gains.astype(F32) + pack[8:16].astype(F32)
    weights = pick(mine, y_lo).astype(F32) + pack[16:].astype(F32)
    return weights, coarse, gains[:2]


def pack_units(big, coarse, gains):
    x, core, *_ = position()
    padded = jnp.concatenate([gains, jnp.zeros((14, WIDTH), gains.dtype)], axis=0).astype(BF16)
    big = big.reshape(4, 2, 2, 224, WIDTH).astype(BF16)
    coarse = coarse.reshape(4, 2, 2, 64, WIDTH).astype(BF16)
    gain = jnp.broadcast_to(padded, (4, 2, 2, 16, WIDTH))
    units = jnp.concatenate([big, coarse, gain], axis=3)
    parts = []
    for half, offsets in ((0, (0, 1, 3, 2)), (1, (0, 3, 1, 2))):
        order = jnp.stack([x ^ offset for offset in offsets])
        parts.append(jnp.take(units[:, :, half], order, axis=0))
    units = jnp.stack(parts)
    keep = lax.dynamic_index_in_dim(units, core, 2, keepdims=False)
    send = lax.dynamic_index_in_dim(units, 1 - core, 2, keepdims=False)
    return keep, send


def layer_norm(values, gain):
    center = values - jnp.mean(values, axis=-1, keepdims=True)
    spread = jnp.mean(center * center, axis=-1, keepdims=True)
    return center * lax.rsqrt(spread + 1e-05) * gain


def local_layer(send, recv, live, table, own, edges, w_ein, w_eout, w_nin, w_nout, gain_e, gain_n):
    count = own.shape[0]
    from_send = jnp.take(table, send, axis=0)
    from_recv = jnp.take(own, recv, axis=0)
    joined = jnp.concatenate([from_send, from_recv, edges], axis=-1).astype(jnp.bfloat16)
    hidden = jax.nn.silu(jnp.dot(joined, w_ein, preferred_element_type=jnp.float32)).astype(
        jnp.bfloat16
    )
    message = layer_norm(jnp.dot(hidden, w_eout, preferred_element_type=jnp.float32), gain_e)
    new_edge = (edges + message).astype(jnp.bfloat16)
    pooled = jax.ops.segment_sum(
        message * live[:, None].astype(jnp.float32), recv, num_segments=count
    )
    node_input = jnp.concatenate([own, pooled], axis=-1).astype(jnp.bfloat16)
    node_hidden = jax.nn.silu(
        jnp.dot(node_input, w_nin, preferred_element_type=jnp.float32)
    ).astype(jnp.bfloat16)
    update = layer_norm(jnp.dot(node_hidden, w_nout, preferred_element_type=jnp.float32), gain_n)
    new_node = (own + update).astype(jnp.bfloat16)
    return (new_node, new_edge)


def on_device(
    node_latent,
    edge_latent,
    senders,
    receivers,
    edge_live,
    halo_list,
    coarse_list,
    edge_in_w,
    edge_out_w,
    node_in_w,
    node_out_w,
    edge_gain,
    node_gain,
    node_cot,
    edge_cot,
):
    nodes_bf = node_latent[0, 0, 0]
    own = nodes_bf.astype(jnp.float32)
    edges32 = edge_latent[0, 0, 0].astype(jnp.float32)
    send = senders[0, 0]
    recv = receivers[0, 0]
    live = edge_live[0, 0]
    rim_list = halo_list[0, 0]
    coarse_ids = coarse_list[0, 0]
    count = own.shape[0]
    rim_rows = rim_list.shape[0]
    outgoing = jnp.take(nodes_bf, rim_list, axis=0)
    received = []
    for step_by in (1, -1):
        received.append(shifted(outgoing, "lat", step_by))
    for step_by in (1, -1):
        received.append(from_behind(outgoing, "lon", step_by))
    coarse_own = jnp.take(nodes_bf, coarse_ids, axis=0)
    coarse_all = gather_coarse(coarse_own)
    first = count + 4 * rim_rows
    slot = jnp.where(send >= first, first + coarse_slot(send - first), send)
    table = jnp.concatenate(
        [own]
        + [piece.astype(jnp.float32) for piece in received]
        + [coarse_all.astype(jnp.float32)],
        axis=0,
    )
    layer = functools.partial(local_layer, slot, recv, live)
    primal, pullback = jax.vjp(
        layer,
        table,
        own,
        edges32,
        edge_in_w,
        edge_out_w,
        node_in_w,
        node_out_w,
        edge_gain,
        node_gain,
    )
    grads = pullback((node_cot[0, 0, 0], edge_cot[0, 0, 0]))
    table_grad = grads[0]
    own_grad = grads[1] + table_grad[:count]
    rim_grads = [table_grad[count + k * rim_rows : count + (k + 1) * rim_rows] for k in range(4)]
    returned = jnp.zeros((rim_rows, own.shape[1]), jnp.float32)
    for step_by, piece in ((1, rim_grads[0]), (-1, rim_grads[1])):
        returned = returned + shifted(piece.astype(jnp.bfloat16), "lat", -step_by).astype(
            piece.dtype
        )
    for step_by, piece in ((1, rim_grads[2]), (-1, rim_grads[3])):
        returned = returned + from_behind(piece.astype(jnp.bfloat16), "lon", -step_by).astype(
            piece.dtype
        )
    own_grad = own_grad + jax.ops.segment_sum(returned, rim_list, num_segments=count)
    coarse_grad_all = jnp.take(
        table_grad[count + 4 * rim_rows :], coarse_slot(jnp.arange(1024, dtype=jnp.int32)), axis=0
    )
    devices = lax.axis_size("lat") * lax.axis_size("lon") * lax.axis_size("dp")
    factor = 1.0 / jnp.sqrt(jnp.float32(send.shape[0] * devices))
    big = jnp.concatenate([grads[3], grads[4], grads[5], grads[6]], axis=0)
    keep, away = pack_units(big, coarse_grad_all, jnp.stack([grads[7], grads[8]]))
    weight_share, coarse_mine, gain_sums = reduce_all(keep, away)
    own_grad = own_grad + jax.ops.segment_sum(coarse_mine, coarse_ids, num_segments=count)
    weight_share = weight_share.reshape(-1)
    gain_grad = gain_sums * factor
    new_nodes = primal[0][None, None, None]
    new_edges = primal[1][None, None, None]
    node_grad = own_grad.astype(jnp.bfloat16)[None, None, None]
    edge_grad = grads[2].astype(jnp.bfloat16)[None, None, None]
    return (new_nodes, new_edges, node_grad, edge_grad, weight_share * factor, gain_grad)


def solution(mesh):
    placed = (
        P("dp", "lat", "lon", None, None),
        P("dp", "lat", "lon", None, None),
        P("lat", "lon", None),
        P("lat", "lon", None),
        P("lat", "lon", None),
        P("lat", "lon", None),
        P("lat", "lon", None),
        P(),
        P(),
        P(),
        P(),
        P(),
        P(),
        P("dp", "lat", "lon", None, None),
        P("dp", "lat", "lon", None, None),
    )
    return jax.shard_map(
        on_device,
        mesh=mesh,
        in_specs=placed,
        out_specs=(
            P("dp", "lat", "lon", None, None),
            P("dp", "lat", "lon", None, None),
            P("dp", "lat", "lon", None, None),
            P("dp", "lat", "lon", None, None),
            P(("lat", "lon", "dp")),
            P(),
        ),
        check_vma=False,
    )
```

```python
import functools
import math

import jax
import jax.numpy as jnp
from jax import lax
from jax.experimental import pallas as pl
from jax.experimental.pallas import tpu as pltpu
from jax.sharding import PartitionSpec as P

AXES = ("lat", "lon", "dp")
F32 = jnp.float32
BF16 = jnp.bfloat16
WIDTH = 512
UNIT = 304


def shifted(block, axis, distance):
    devices = range(lax.axis_size(axis))
    route = [(i - distance, i) for i in devices if i - distance in devices]
    return lax.ppermute(block, axis, route)


def from_behind(value, axis, steps):
    count = lax.axis_size(axis)
    pairs = [(source, (source + steps) % count) for source in range(count)]
    return lax.ppermute(value, axis, pairs)


def partner_of(index, kind, amount):
    x, core, z = index >> 6, index >> 5 & 1, index >> 2 & 7
    y_lo, y_hi = index >> 1 & 1, index & 1
    if kind == "core":
        core ^= 1
    elif kind == "x":
        x ^= amount
    elif kind == "z":
        z ^= amount
    elif kind == "ring":
        z = (z - amount if z & 1 else z + amount) & 7
    elif kind == "y":
        y_lo ^= amount & 1
        y_hi ^= amount >> 1
    return ((x * 2 + core) * 8 + z) * 4 + y_lo * 2 + y_hi


def exchange(value, kind, amount=1):
    pairs = [(i, partner_of(i, kind, amount)) for i in range(256)]
    return lax.ppermute(value, AXES, pairs)


def position():
    lat, lon, dp = (lax.axis_index(axis) for axis in AXES)
    return lat >> 1, lat & 1, lon >> 1, lon & 1, dp


def doubled(rows, *stages):
    for kind, amount in stages:
        rows = jnp.concatenate([rows, exchange(rows, kind, amount)], axis=0)
    return rows


def coarse_slot(row):
    x, core, z, y_lo, _ = position()
    owner, within = row >> 3, row & 7
    dx = (owner >> 5) ^ x
    dcore = (owner >> 4 & 1) ^ core
    ahead = ((owner >> 1 & 7) - z) * (1 - 2 * (z & 1)) & 7
    zslot = 0x23764510 >> (4 * ahead) & 7
    dy = (owner & 1) ^ y_lo
    high, mixed = dx >> 1, (dx ^ dx >> 1) & 1
    half = zslot >> 2
    xslot = jnp.where(half == 0, high * 2 + mixed, mixed * 2 + high)
    return dcore * 512 + half * 256 + xslot * 64 + (zslot & 3) * 16 + dy * 8 + within


def plus(*values):
    total = values[0].astype(F32)
    for value in values[1:]:
        total = lax.reduce_precision(total + value.astype(F32), 8, 7)
    return total.astype(BF16)


def pick(array, which, axis=0):
    return lax.dynamic_index_in_dim(array, which, axis, keepdims=False)


def reduce_all(keep_far, send_far, keep_near, send_near, rim_grad):
    _, _, z, y_lo, y_hi = position()
    got_far = exchange(send_far, "core")
    got_near = exchange(send_near, "core")
    got_a = exchange(plus(keep_far[0], got_far[0]), "x", 3)
    got_b = exchange(plus(keep_far[1], got_far[1]), "x", 1)
    back_lon = [from_behind(rim_grad[128 * k : 128 * k + 128], "lon", step) for k, step in ((2, -1), (3, 1))]
    got_a, got_b, *back_lon = lax.optimization_barrier((got_a, got_b, *back_lon))
    new_a = exchange(plus(keep_near[0, 1], got_near[0, 1], got_a[1]), "x", 1)
    new_b = exchange(plus(keep_near[1, 1], got_near[1, 1], got_b[1]), "x", 3)
    new_a, new_b, rim_grad = lax.optimization_barrier((new_a, new_b, rim_grad))
    back_lat = [shifted(rim_grad[128 * k : 128 * k + 128], "lat", step) for k, step in ((0, -1), (1, 1))]
    a = plus(keep_near[0, 0], got_near[0, 0], got_a[0], new_a)
    b = plus(keep_near[1, 0], got_near[1, 0], got_b[0], new_b)
    weights = jnp.concatenate([a[:224], b[:224]], axis=0).reshape(8, 4, 14, WIDTH)
    gains = jnp.broadcast_to(a[288:290], (8, 4, 2, WIDTH))
    coarse = jnp.concatenate([a[224:288], b[224:288]], axis=0).reshape(8, 2, 8, WIDTH)
    units = jnp.concatenate([weights, gains], axis=2).reshape(8, 2, 2, 16, WIDTH)
    got = exchange(pick(units, 1 - y_hi, 2), "y", 3)
    units = plus(pick(units, y_hi, 2), got)
    units = jnp.concatenate([units, coarse], axis=2)
    got = exchange(pick(units, 1 - y_lo, 1), "y", 1)
    units = plus(pick(units, y_lo, 1), got).reshape(2, 2, 2, 24, WIDTH)
    units, *back_lat = lax.optimization_barrier((units, *back_lat))
    got = exchange(pick(units, 1 - (z & 1), 2), "z", 1)
    units = plus(pick(units, z & 1, 2), got)
    got = exchange(pick(units, 1 - (z >> 1 & 1), 1), "z", 2)
    units = plus(pick(units, z >> 1 & 1, 1), got)
    got = exchange(pick(units, 1 - (z >> 2)), "z", 4)
    return pick(units, z >> 2), got, back_lat + back_lon


def dot(a, b, ca=1, cb=0):
    return lax.dot_general(a, b, (((ca,), (cb,)), ((), ())), preferred_element_type=F32)


def down(row, count):
    return jnp.broadcast_to(row, (128, count)).T


def one_hot(columns, first, width):
    lane = lax.broadcasted_iota(jnp.int32, columns.shape, 1)
    tiles = [columns == lane + (first + at) for at in range(0, width, 128)]
    return jnp.concatenate([tile.astype(F32).astype(BF16) for tile in tiles], axis=1)


def one_hot_t(row, first, height):
    at = lax.broadcasted_iota(jnp.int32, (height, row.shape[1]), 0) + first
    return (at == row).astype(F32).astype(BF16)


def normed(values):
    center = values - jnp.mean(values, axis=-1, keepdims=True)
    spread = jnp.mean(center * center, axis=-1, keepdims=True)
    scale = lax.rsqrt(spread + 1e-05)
    return center * scale, scale


def normed_back(grad, unit, scale):
    inner = jnp.mean(grad * unit, axis=-1, keepdims=True)
    return scale * (grad - jnp.mean(grad, axis=-1, keepdims=True) - unit * inner)


def silu_slope(pre):
    gate = jax.nn.sigmoid(pre)
    return gate * (1.0 + pre * (1.0 - gate))


def outgoing_kernel(rim_ref, coarse_ref, nodes_ref, rows_ref, coarse_rows_ref):
    nodes = nodes_ref[...]
    rows_ref[...] = dot(one_hot(down(rim_ref[...], 128), 0, 256), nodes).astype(BF16)
    coarse_rows_ref[...] = dot(one_hot_t(coarse_ref[...], 0, 256), nodes, 0, 0).astype(BF16)


def fetch(pairs, sems):
    copies = [pltpu.make_async_copy(src, dst, sems.at[n]) for n, (src, dst) in enumerate(pairs)]
    for copy in copies:
        copy.start()
    return lambda n: copies[n].wait()


def near_kernel(
    index_ref,
    nodes_hbm,
    edges_hbm,
    w_ein_hbm,
    w_nin_hbm,
    pre_ref,
    node_pre_ref,
    recv_rows_ref,
    own_rows_ref,
    nodes_ref,
    edges_ref,
    w_ein_ref,
    w_nin_ref,
    sems,
):
    wait = fetch(
        (
            (nodes_hbm, nodes_ref),
            (w_ein_hbm, w_ein_ref),
            (edges_hbm, edges_ref),
            (w_nin_hbm.at[0:512], w_nin_ref),
        ),
        sems,
    )
    slots = one_hot(down(index_ref[0:1], 384), 0, 256)
    receivers = one_hot(down(index_ref[2:3], 384), 0, 256)
    wait(0)
    nodes = nodes_ref[...]
    recv_rows = dot(receivers, nodes).astype(BF16)
    own_rows = dot(slots, nodes).astype(BF16)
    recv_rows_ref[...] = recv_rows
    own_rows_ref[...] = own_rows
    wait(1)
    wait(2)
    pre_ref[...] = (
        dot(own_rows, w_ein_ref[0:512])
        + dot(recv_rows, w_ein_ref[512:1024])
        + dot(edges_ref[...], w_ein_ref[1024:1536])
    )
    wait(3)
    node_pre_ref[...] = dot(nodes, w_nin_ref[...])


def layer_kernel(
    place_ref,
    index_ref,
    pre_ref,
    node_pre_ref,
    recv_rows_ref,
    own_rows_ref,
    edges_hbm,
    nodes_hbm,
    lower_ref,
    upper_ref,
    west_ref,
    east_ref,
    near_top_ref,
    near_low_ref,
    far_top_ref,
    far_low_ref,
    w_ein_hbm,
    w_eout_hbm,
    w_nin_hbm,
    w_nout_hbm,
    gain_e_ref,
    gain_n_ref,
    node_cot_hbm,
    edge_cot_hbm,
    new_nodes_hbm,
    new_edges_hbm,
    edge_grad_hbm,
    own_grad_hbm,
    rim_grad_ref,
    keep_far_ref,
    send_far_ref,
    keep_near_ref,
    send_near_ref,
    big_ref,
    coarse_ref,
    unit_ref,
    edges_ref,
    nodes_ref,
    w_ein_ref,
    w_eout_ref,
    w_nin_ref,
    w_nout_ref,
    node_cot_ref,
    edge_cot_ref,
    new_nodes_ref,
    new_edges_ref,
    edge_grad_ref,
    own_grad_ref,
    sems,
    out_sems,
):
    wait = fetch(
        (
            (w_ein_hbm, w_ein_ref),
            (w_eout_hbm, w_eout_ref),
            (edges_hbm, edges_ref),
            (w_nin_hbm, w_nin_ref),
            (w_nout_hbm, w_nout_ref),
            (nodes_hbm, nodes_ref),
            (node_cot_hbm, node_cot_ref),
            (edge_cot_hbm, edge_cot_ref),
        ),
        sems,
    )
    slots = down(index_ref[0:1], 384)
    lower_upper = jnp.concatenate([lower_ref[...], upper_ref[...]], axis=0)
    west_east = jnp.concatenate([west_ref[...], east_ref[...]], axis=0)
    far = (
        dot(one_hot(slots, 256, 256), lower_upper)
        + dot(one_hot(slots, 512, 256), west_east)
        + dot(one_hot(slots, 768, 256), near_top_ref[...])
        + dot(one_hot(slots, 1024, 256), near_low_ref[...])
        + dot(one_hot(slots, 1280, 256), far_top_ref[...])
        + dot(one_hot(slots, 1536, 256), far_low_ref[...])
    ).astype(BF16)
    send_rows = (far.astype(F32) + own_rows_ref[...].astype(F32)).astype(BF16)
    wait(0)
    pre = pre_ref[...] + dot(far, w_ein_ref[0:512])
    hidden = (pre * jax.nn.sigmoid(pre)).astype(BF16)
    gain_e = gain_e_ref[...]
    wait(1)
    unit, scale = normed(dot(hidden, w_eout_ref[...]))
    unit_ref[...] = unit
    message = unit * gain_e
    wait(2)
    new_edges_ref[...] = (edges_ref[...].astype(F32) + message).astype(BF16)
    new_edges_out = pltpu.make_async_copy(new_edges_ref, new_edges_hbm, out_sems.at[0])
    new_edges_out.start()
    into = one_hot_t(index_ref[3:4], 0, 256)
    coarse_part = message.astype(BF16)
    fine_part = (message - coarse_part.astype(F32)).astype(BF16)
    pooled = (dot(into, coarse_part) + dot(into, fine_part)).astype(BF16)
    for n in (3, 4, 5, 6, 7):
        wait(n)
    nodes = nodes_ref[...]
    gain_n = gain_n_ref[...]
    node_pre = node_pre_ref[...] + dot(pooled, w_nin_ref[512:1024])
    node_hidden = (node_pre * jax.nn.sigmoid(node_pre)).astype(BF16)
    node_unit, node_scale = normed(dot(node_hidden, w_nout_ref[...]))
    new_nodes_ref[...] = (nodes.astype(F32) + node_unit * gain_n).astype(BF16)
    new_nodes_out = pltpu.make_async_copy(new_nodes_ref, new_nodes_hbm, out_sems.at[1])
    new_nodes_out.start()
    node_cot = node_cot_ref[...].astype(F32)
    gain_grad_n = jnp.sum(node_cot * node_unit, axis=0, keepdims=True)
    back = normed_back(node_cot * gain_n, node_unit, node_scale).astype(BF16)
    big_ref[3072:3584] = dot(node_hidden, back, 0, 0).astype(BF16)
    back = dot(back, w_nout_ref[...], 1, 1).astype(BF16).astype(F32)
    back = (back * silu_slope(node_pre)).astype(BF16)
    big_ref[2048:2560] = dot(nodes, back, 0, 0).astype(BF16)
    big_ref[2560:3072] = dot(pooled, back, 0, 0).astype(BF16)
    own_grad = node_cot + dot(back, w_nin_ref[0:512], 1, 1).astype(BF16).astype(F32)
    pooled_grad = dot(back, w_nin_ref[512:1024], 1, 1).astype(BF16)
    edge_cot = edge_cot_ref[...].astype(F32)
    grad = edge_cot + dot(one_hot(down(index_ref[3:4], 384), 0, 256), pooled_grad)
    unit = unit_ref[...]
    gain_grad_e = jnp.sum(grad * unit, axis=0, keepdims=True)
    back = normed_back(grad * gain_e, unit, scale).astype(BF16)
    big_ref[1536:2048] = dot(hidden, back, 0, 0).astype(BF16)
    back = dot(back, w_eout_ref[...], 1, 1).astype(BF16).astype(F32)
    back = (back * silu_slope(pre)).astype(BF16)
    send_grad = dot(back, w_ein_ref[0:512], 1, 1).astype(BF16)
    recv_grad = dot(back, w_ein_ref[512:1024], 1, 1).astype(BF16)
    big_ref[0:512] = dot(send_rows, back, 0, 0).astype(BF16)
    big_ref[512:1024] = dot(recv_rows_ref[...], back, 0, 0).astype(BF16)
    big_ref[1024:1536] = dot(edges_ref[...], back, 0, 0).astype(BF16)
    edge_grad_ref[...] = (
        edge_cot + dot(back, w_ein_ref[1024:1536], 1, 1).astype(BF16).astype(F32)
    ).astype(BF16)
    edge_grad_out = pltpu.make_async_copy(edge_grad_ref, edge_grad_hbm, out_sems.at[2])
    edge_grad_out.start()
    senders = index_ref[1:2]
    own_grad_ref[...] = (
        own_grad
        + dot(one_hot_t(index_ref[2:3], 0, 256), recv_grad)
        + dot(one_hot_t(senders, 0, 256), send_grad)
    )
    own_grad_out = pltpu.make_async_copy(own_grad_ref, own_grad_hbm, out_sems.at[3])
    own_grad_out.start()
    rim_grad_ref[...] = dot(one_hot_t(senders, 256, 512), send_grad).astype(BF16)
    coarse_ref[...] = dot(one_hot_t(senders, 768, 1024), send_grad).astype(BF16)
    row = lax.broadcasted_iota(jnp.int32, (16, WIDTH), 0)
    gains = jnp.where(row == 0, gain_grad_e, jnp.where(row == 1, gain_grad_n, 0.0)).astype(BF16)
    x, core = place_ref[0], place_ref[1]
    for half, offsets in ((0, (0, 1, 3, 2)), (1, (0, 3, 1, 2))):
        for at, offset in enumerate(offsets):
            sides = (keep_far_ref, send_far_ref) if at >= 2 else (keep_near_ref, send_near_ref)
            for ref, other in zip(sides, (core, 1 - core)):
                block = (x ^ offset) * 2 + other
                rows = pl.ds(pl.multiple_of(block * 448 + half * 224, 32), 224)
                ref[half, at % 2, 0:224] = big_ref[rows]
                rows = pl.ds(pl.multiple_of(block * 128 + half * 64, 64), 64)
                ref[half, at % 2, 224:288] = coarse_ref[rows]
                ref[half, at % 2, 288:304] = gains
    for copy in (new_edges_out, new_nodes_out, edge_grad_out, own_grad_out):
        copy.wait()


def finish_kernel(
    factor, rim_ref, coarse_ref, own_ref, a_ref, b_ref, c_ref, d_ref, kept_ref, got_ref, out_ref, weights_ref, gains_ref, sum_ref
):
    into = one_hot_t(rim_ref[...], 0, 256)
    total = own_ref[...] + dot(into, a_ref[...]) + dot(into, b_ref[...])
    total = total + dot(into, c_ref[...]) + dot(into, d_ref[...])
    sum_ref[...] = kept_ref[...].astype(F32) + got_ref[...].astype(F32)
    weights_ref[...] = sum_ref[0:14] * factor
    gains_ref[...] = sum_ref[14:16] * factor
    at = lax.broadcasted_iota(jnp.int32, (256, 8), 0)
    coarse_into = (at == coarse_ref[...]).astype(F32)
    total = total + lax.dot_general(
        coarse_into,
        sum_ref[16:24],
        (((1,), (0,)), ((), ())),
        precision=lax.Precision.HIGHEST,
        preferred_element_type=F32,
    )
    out_ref[...] = total.astype(BF16)


def call(kernel, out, *operands, scratch=(), small=(), there=(), out_there=(), flops=0, limit=48):
    def spec(at, away):
        return pl.BlockSpec(memory_space=pltpu.SMEM if at in small else pltpu.HBM if at in away else pltpu.VMEM)

    size = sum(value.size * value.dtype.itemsize for value in operands)
    size += sum(math.prod(shape) * jnp.dtype(dtype).itemsize for shape, dtype in out)
    return pl.pallas_call(
        kernel,
        out_shape=[jax.ShapeDtypeStruct(*leaf) for leaf in out],
        in_specs=[spec(at, there) for at in range(len(operands))],
        out_specs=[pl.BlockSpec(memory_space=pltpu.HBM if at in out_there else pltpu.VMEM) for at in range(len(out))],
        scratch_shapes=list(scratch),
        compiler_params=pltpu.CompilerParams(vmem_limit_bytes=limit * 1024 * 1024),
        cost_estimate=pl.CostEstimate(flops=flops, bytes_accessed=size, transcendentals=0),
    )(*operands)


def on_device(
    node_latent,
    edge_latent,
    senders,
    receivers,
    edge_live,
    halo_list,
    coarse_list,
    edge_in_w,
    edge_out_w,
    node_in_w,
    node_out_w,
    edge_gain,
    node_gain,
    node_cot,
    edge_cot,
):
    nodes, edges = node_latent[0, 0, 0], edge_latent[0, 0, 0]
    send, recv = senders[0], receivers[0]
    rim_list, coarse_ids = halo_list[0], coarse_list[0]
    x, core, *_ = position()
    outgoing, coarse_own = call(
        outgoing_kernel,
        [((128, WIDTH), BF16), ((8, WIDTH), BF16)],
        rim_list,
        coarse_ids,
        nodes,
        flops=2 * 136 * 256 * 512,
        limit=16,
    )
    rims = [shifted(outgoing, "lat", step) for step in (1, -1)]
    slot = jnp.where(send >= 768, 768 + coarse_slot(send - 768), send)
    live_recv = jnp.where(edge_live[0] != 0, recv, -1)
    index = jnp.concatenate([slot, send, recv, live_recv, slot, slot, slot, slot], axis=0)
    pre, node_pre, recv_rows, own_rows = call(
        near_kernel,
        [((384, WIDTH), F32), ((256, WIDTH), F32), ((384, WIDTH), BF16), ((384, WIDTH), BF16)],
        index,
        nodes,
        edges,
        edge_in_w,
        node_in_w,
        scratch=[
            pltpu.VMEM((256, WIDTH), BF16),
            pltpu.VMEM((384, WIDTH), BF16),
            pltpu.VMEM((1536, WIDTH), BF16),
            pltpu.VMEM((512, WIDTH), BF16),
            pltpu.SemaphoreType.DMA((4,)),
        ],
        there=(1, 2, 3, 4),
        flops=2 * 384 * 2048 * 512,
        limit=24,
    )
    rows = doubled(coarse_own, ("y", 1), ("ring", 1), ("ring", -1))
    rows, *rims = lax.optimization_barrier((rows, *rims))
    rows = doubled(rows, ("ring", 3))
    rows, outgoing, pre, node_pre, recv_rows, own_rows = lax.optimization_barrier(
        (rows, outgoing, pre, node_pre, recv_rows, own_rows)
    )
    top, low = doubled(rows[:64], ("x", 1)), doubled(rows[64:], ("x", 3))
    rims += [from_behind(outgoing, "lon", step) for step in (1, -1)]
    top, low, *rims = lax.optimization_barrier((top, low, *rims))
    gathered = [doubled(top, ("x", 3)), doubled(low, ("x", 1))]
    gathered += [exchange(rows, "core") for rows in gathered]
    place = jnp.stack([x, core]).astype(jnp.int32)
    new_nodes, new_edges, edge_grad, own_grad, rim_grad, *units = call(
        layer_kernel,
        [
            ((256, WIDTH), BF16),
            ((384, WIDTH), BF16),
            ((384, WIDTH), BF16),
            ((256, WIDTH), F32),
            ((512, WIDTH), BF16),
            ((2, 2, UNIT, WIDTH), BF16),
            ((2, 2, UNIT, WIDTH), BF16),
            ((2, 2, UNIT, WIDTH), BF16),
            ((2, 2, UNIT, WIDTH), BF16),
        ],
        place,
        index,
        pre,
        node_pre,
        recv_rows,
        own_rows,
        edges,
        nodes,
        *rims,
        *gathered,
        edge_in_w,
        edge_out_w,
        node_in_w,
        node_out_w,
        edge_gain[None],
        node_gain[None],
        node_cot[0, 0, 0],
        edge_cot[0, 0, 0],
        scratch=[
            pltpu.VMEM((3584, WIDTH), BF16),
            pltpu.VMEM((1024, WIDTH), BF16),
            pltpu.VMEM((384, WIDTH), F32),
            pltpu.VMEM((384, WIDTH), BF16),
            pltpu.VMEM((256, WIDTH), BF16),
            pltpu.VMEM((1536, WIDTH), BF16),
            pltpu.VMEM((512, WIDTH), BF16),
            pltpu.VMEM((1024, WIDTH), BF16),
            pltpu.VMEM((512, WIDTH), BF16),
            pltpu.VMEM((256, WIDTH), BF16),
            pltpu.VMEM((384, WIDTH), BF16),
            pltpu.VMEM((256, WIDTH), BF16),
            pltpu.VMEM((384, WIDTH), BF16),
            pltpu.VMEM((384, WIDTH), BF16),
            pltpu.VMEM((256, WIDTH), F32),
            pltpu.SemaphoreType.DMA((8,)),
            pltpu.SemaphoreType.DMA((4,)),
        ],
        small=(0,),
        there=(6, 7, 16, 17, 18, 19, 22, 23),
        out_there=(0, 1, 2, 3),
        flops=2 * 384 * 512 * 10000,
    )
    kept, got, back = reduce_all(*units, rim_grad)
    devices = lax.axis_size("lat") * lax.axis_size("lon") * lax.axis_size("dp")
    node_grad, weight_share, gain_grad = call(
        functools.partial(finish_kernel, 1.0 / math.sqrt(384 * devices)),
        [((256, WIDTH), BF16), ((14, WIDTH), F32), ((2, WIDTH), F32)],
        rim_list,
        coarse_ids,
        own_grad,
        *back,
        kept,
        got,
        scratch=[pltpu.VMEM((24, WIDTH), F32)],
        flops=2 * 512 * 256 * 512,
        limit=16,
    )
    wrap = (None, None, None)
    return (
        new_nodes[wrap],
        new_edges[wrap],
        node_grad[wrap],
        edge_grad[wrap],
        weight_share.reshape(-1),
        gain_grad,
    )


def solution(mesh):
    placed = (
        P("dp", "lat", "lon", None, None),
        P("dp", "lat", "lon", None, None),
        P("lat", "lon", None),
        P("lat", "lon", None),
        P("lat", "lon", None),
        P("lat", "lon", None),
        P("lat", "lon", None),
        P(),
        P(),
        P(),
        P(),
        P(),
        P(),
        P("dp", "lat", "lon", None, None),
        P("dp", "lat", "lon", None, None),
    )
    return jax.shard_map(
        on_device,
        mesh=mesh,
        in_specs=placed,
        out_specs=(
            P("dp", "lat", "lon", None, None),
            P("dp", "lat", "lon", None, None),
            P("dp", "lat", "lon", None, None),
            P("dp", "lat", "lon", None, None),
            P(("lat", "lon", "dp")),
            P(),
        ),
        check_vma=False,
    )
```

```python
import functools
import math

import jax
import jax.numpy as jnp
from jax import lax
from jax.experimental import pallas as pl
from jax.experimental.pallas import tpu as pltpu
from jax.sharding import PartitionSpec as P

AXES = ("lat", "lon", "dp")
F32 = jnp.float32
BF16 = jnp.bfloat16
WIDTH = 512
UNIT = 304


def partner_of(index, kind, amount):
    x, core, z = index >> 6, index >> 5 & 1, index >> 2 & 7
    y_lo, y_hi = index >> 1 & 1, index & 1
    if kind == "core":
        core ^= 1
    elif kind == "x":
        x ^= amount
    elif kind == "z":
        z ^= amount
    elif kind == "ring":
        z = (z - amount if z & 1 else z + amount) & 7
    elif kind == "y":
        y_lo ^= amount & 1
        y_hi ^= amount >> 1
    elif kind == "next band":
        x, core = x + (2 * core - 1), 1 - core
        if not 0 <= x < 4:
            return None
    elif kind == "next sector":
        z, y_lo = (z + 2 * y_lo - 1) & 7, 1 - y_lo
    return ((x * 2 + core) * 8 + z) * 4 + y_lo * 2 + y_hi


def exchange(value, kind, amount=1):
    pairs = [(i, partner_of(i, kind, amount)) for i in range(256)]
    return lax.ppermute(value, AXES, [pair for pair in pairs if pair[1] is not None])


def position():
    lat, lon, dp = (lax.axis_index(axis) for axis in AXES)
    return lat >> 1, lat & 1, lon >> 1, lon & 1, dp


def doubled(rows, *stages):
    for kind, amount in stages:
        rows = jnp.concatenate([rows, exchange(rows, kind, amount)], axis=0)
    return rows


def coarse_slot(row):
    x, core, z, y_lo, _ = position()
    owner, within = row >> 3, row & 7
    dx = (owner >> 5) ^ x
    dcore = (owner >> 4 & 1) ^ core
    ahead = ((owner >> 1 & 7) - z) * (1 - 2 * (z & 1)) & 7
    zslot = 0x23764510 >> (4 * ahead) & 7
    dy = (owner & 1) ^ y_lo
    high, mixed = dx >> 1, (dx ^ dx >> 1) & 1
    half = zslot >> 2
    xslot = jnp.where(half == 0, high * 2 + mixed, mixed * 2 + high)
    return dcore * 512 + half * 256 + xslot * 64 + (zslot & 3) * 16 + dy * 8 + within


def rim_slot(row):
    _, core, _, y_lo, _ = position()
    axis, upper = row >> 8, row >> 7 & 1
    block = upper ^ 1 ^ jnp.where(axis == 0, core, y_lo)
    return axis * 256 + block * 128 + (row & 127)


def plus(*values):
    total = values[0].astype(F32)
    for value in values[1:]:
        total = lax.reduce_precision(total + value.astype(F32), 8, 7)
    return total.astype(BF16)


def pick(array, which, axis=0):
    return lax.dynamic_index_in_dim(array, which, axis, keepdims=False)


def reduce_all(rim_grads, keep_far, send_far, keep_near, send_near):
    _, _, z, y_lo, y_hi = position()
    got_far = exchange(send_far, "core")
    to_core, to_band, to_y, to_sector = rim_grads
    back_core = exchange(to_core, "core")
    got_near = exchange(send_near, "core")
    got_a = exchange(plus(keep_far[0], got_far[0]), "x", 3)
    got_b = exchange(plus(keep_far[1], got_far[1]), "x", 1)
    back_band = exchange(to_band, "next band")
    back_sector = exchange(to_sector, "next sector")
    got_a, got_b, to_y, back_core, back_band, back_sector = lax.optimization_barrier(
        (got_a, got_b, to_y, back_core, back_band, back_sector)
    )
    next_a = plus(keep_near[0, 1], got_near[0, 1], got_a[1])
    next_b = plus(keep_near[1, 1], got_near[1, 1], got_b[1])
    next_a, next_b = lax.optimization_barrier((next_a, next_b))
    new_a, new_b = exchange(next_a, "x", 1), exchange(next_b, "x", 3)
    a = plus(keep_near[0, 0], got_near[0, 0], got_a[0], new_a)
    b = plus(keep_near[1, 0], got_near[1, 0], got_b[0], new_b)
    weights = jnp.concatenate([a[:224], b[:224]], axis=0).reshape(8, 4, 14, WIDTH)
    gains = jnp.broadcast_to(a[288:290], (8, 4, 2, WIDTH))
    coarse = jnp.concatenate([a[224:288], b[224:288]], axis=0).reshape(8, 2, 8, WIDTH)
    units = jnp.concatenate([weights, gains], axis=2).reshape(8, 2, 2, 16, WIDTH)
    got = exchange(pick(units, 1 - y_hi, 2), "y", 3)
    units = plus(pick(units, y_hi, 2), got)
    units = jnp.concatenate([units, coarse], axis=2)
    units, to_y = lax.optimization_barrier((units, to_y))
    got = exchange(pick(units, 1 - y_lo, 1), "y", 1)
    back_y = exchange(to_y, "y")
    units = plus(pick(units, y_lo, 1), got).reshape(2, 2, 2, 24, WIDTH)
    got = exchange(pick(units, 1 - (z & 1), 2), "z", 1)
    units = plus(pick(units, z & 1, 2), got)
    got = exchange(pick(units, 1 - (z >> 1 & 1), 1), "z", 2)
    units = plus(pick(units, z >> 1 & 1, 1), got)
    units, back_y = lax.optimization_barrier((units, back_y))
    got = exchange(pick(units, 1 - (z >> 2)), "z", 4)
    return pick(units, z >> 2), got, (back_core, back_band, back_y, back_sector)


def dot(a, b, ca=1, cb=0):
    return lax.dot_general(a, b, (((ca,), (cb,)), ((), ())), preferred_element_type=F32)


def down(row, count):
    return jnp.broadcast_to(row, (128, count)).T


def one_hot(columns, first, width):
    lane = lax.broadcasted_iota(jnp.int32, columns.shape, 1)
    tiles = [columns == lane + (first + at) for at in range(0, width, 128)]
    return jnp.concatenate([tile.astype(F32).astype(BF16) for tile in tiles], axis=1)


def one_hot_t(row, first, height):
    at = lax.broadcasted_iota(jnp.int32, (height, row.shape[1]), 0) + first
    return (at == row).astype(F32).astype(BF16)


def normed(values):
    center = values - jnp.mean(values, axis=-1, keepdims=True)
    spread = jnp.mean(center * center, axis=-1, keepdims=True)
    scale = lax.rsqrt(spread + 1e-05)
    return center * scale, scale


def normed_back(grad, unit, scale):
    inner = jnp.mean(grad * unit, axis=-1, keepdims=True)
    return scale * (grad - jnp.mean(grad, axis=-1, keepdims=True) - unit * inner)


def silu_slope(pre):
    gate = jax.nn.sigmoid(pre)
    return gate * (1.0 + pre * (1.0 - gate))


def outgoing_kernel(rim_ref, coarse_ref, nodes_hbm, rows_ref, coarse_rows_ref, nodes_ref, sems):
    wait = fetch(((nodes_hbm, nodes_ref),), sems)
    rims = one_hot(down(rim_ref[...], 128), 0, 256)
    coarse = one_hot_t(coarse_ref[...], 0, 256)
    wait(0)
    nodes = nodes_ref[...]
    coarse_rows_ref[...] = dot(coarse, nodes, 0, 0).astype(BF16)
    rows_ref[...] = dot(rims, nodes).astype(BF16)


def fetch(pairs, sems):
    copies = [pltpu.make_async_copy(src, dst, sems.at[n]) for n, (src, dst) in enumerate(pairs)]
    for copy in copies:
        copy.start()
    return lambda n: copies[n].wait()


def layer_kernel(
    place_ref,
    index_ref,
    edges_hbm,
    nodes_hbm,
    rim_core_hbm,
    rim_band_hbm,
    rim_y_hbm,
    rim_sector_hbm,
    near_top_hbm,
    near_low_hbm,
    far_top_hbm,
    far_low_hbm,
    w_ein_hbm,
    w_eout_hbm,
    w_nin_hbm,
    w_nout_hbm,
    gain_e_ref,
    gain_n_ref,
    node_cot_hbm,
    edge_cot_hbm,
    new_nodes_hbm,
    new_edges_hbm,
    edge_grad_hbm,
    own_grad_hbm,
    to_core_ref,
    to_band_ref,
    to_y_ref,
    to_sector_ref,
    keep_far_hbm,
    send_far_hbm,
    keep_near_hbm,
    send_near_hbm,
    big_ref,
    coarse_ref,
    unit_ref,
    edges_ref,
    nodes_ref,
    w_ein_ref,
    w_eout_ref,
    w_nin_ref,
    w_nout_ref,
    node_cot_ref,
    edge_cot_ref,
    new_nodes_ref,
    new_edges_ref,
    edge_grad_ref,
    own_grad_ref,
    far_rows_ref,
    gains_ref,
    move_sems,
    coarse_sems,
    sems,
    out_sems,
):
    pieces = (rim_core_hbm, rim_band_hbm, rim_y_hbm, rim_sector_hbm, near_top_hbm, near_low_hbm, far_top_hbm, far_low_hbm)
    starts = (0, 128, 256, 384, 512, 768, 1024, 1280, 1536)
    wait = fetch(
        (
            *[(piece, far_rows_ref.at[lo:hi]) for piece, lo, hi in zip(pieces, starts, starts[1:])],
            (nodes_hbm, nodes_ref),
            (w_ein_hbm, w_ein_ref),
            (edges_hbm, edges_ref),
            (w_eout_hbm, w_eout_ref),
            (w_nin_hbm, w_nin_ref),
            (w_nout_hbm, w_nout_ref),
            (node_cot_hbm, node_cot_ref),
            (edge_cot_hbm, edge_cot_ref),
        ),
        sems,
    )
    slots = down(index_ref[0:1], 384)
    receivers = one_hot(down(index_ref[2:3], 384), 0, 256)
    near = one_hot(slots, 0, 256)
    far = one_hot(slots, 256, 1536)
    for n in range(9):
        wait(n)
    nodes = nodes_ref[...]
    send_rows = (dot(far, far_rows_ref[...]) + dot(near, nodes)).astype(BF16)
    recv_rows = dot(receivers, nodes).astype(BF16)
    wait(9)
    wait(10)
    pre = (
        dot(send_rows, w_ein_ref[0:512])
        + dot(recv_rows, w_ein_ref[512:1024])
        + dot(edges_ref[...], w_ein_ref[1024:1536])
    )
    hidden = (pre * jax.nn.sigmoid(pre)).astype(BF16)
    gain_e = gain_e_ref[...]
    wait(11)
    unit, scale = normed(dot(hidden, w_eout_ref[...]))
    unit_ref[...] = unit
    message = unit * gain_e
    new_edges_ref[...] = (edges_ref[...].astype(F32) + message).astype(BF16)
    new_edges_out = pltpu.make_async_copy(new_edges_ref, new_edges_hbm, out_sems.at[0])
    new_edges_out.start()
    into = one_hot_t(index_ref[3:4], 0, 256)
    coarse_part = message.astype(BF16)
    fine_part = (message - coarse_part.astype(F32)).astype(BF16)
    pooled = (dot(into, coarse_part) + dot(into, fine_part)).astype(BF16)
    for n in (12, 13, 14, 15):
        wait(n)
    gain_n = gain_n_ref[...]
    node_pre = dot(nodes, w_nin_ref[0:512]) + dot(pooled, w_nin_ref[512:1024])
    node_hidden = (node_pre * jax.nn.sigmoid(node_pre)).astype(BF16)
    node_unit, node_scale = normed(dot(node_hidden, w_nout_ref[...]))
    new_nodes_ref[...] = (nodes.astype(F32) + node_unit * gain_n).astype(BF16)
    new_nodes_out = pltpu.make_async_copy(new_nodes_ref, new_nodes_hbm, out_sems.at[1])
    new_nodes_out.start()
    node_cot = node_cot_ref[...].astype(F32)
    gain_grad_n = jnp.sum(node_cot * node_unit, axis=0, keepdims=True)
    back = normed_back(node_cot * gain_n, node_unit, node_scale).astype(BF16)
    big_ref[3072:3584] = dot(node_hidden, back, 0, 0).astype(BF16)
    back = dot(back, w_nout_ref[...], 1, 1).astype(BF16).astype(F32)
    back = (back * silu_slope(node_pre)).astype(BF16)
    big_ref[2048:2560] = dot(nodes, back, 0, 0).astype(BF16)
    big_ref[2560:3072] = dot(pooled, back, 0, 0).astype(BF16)
    own_grad = node_cot + dot(back, w_nin_ref[0:512], 1, 1).astype(BF16).astype(F32)
    pooled_grad = dot(back, w_nin_ref[512:1024], 1, 1).astype(BF16)
    edge_cot = edge_cot_ref[...].astype(F32)
    grad = edge_cot + dot(one_hot(down(index_ref[3:4], 384), 0, 256), pooled_grad)
    unit = unit_ref[...]
    gain_grad_e = jnp.sum(grad * unit, axis=0, keepdims=True)
    back = normed_back(grad * gain_e, unit, scale).astype(BF16)
    big_ref[1536:2048] = dot(hidden, back, 0, 0).astype(BF16)
    back = dot(back, w_eout_ref[...], 1, 1).astype(BF16).astype(F32)
    back = (back * silu_slope(pre)).astype(BF16)
    big_ref[0:512] = dot(send_rows, back, 0, 0).astype(BF16)
    big_ref[512:1024] = dot(recv_rows, back, 0, 0).astype(BF16)
    big_ref[1024:1536] = dot(edges_ref[...], back, 0, 0).astype(BF16)
    row = lax.broadcasted_iota(jnp.int32, (16, WIDTH), 0)
    gains = jnp.where(row == 0, gain_grad_e, jnp.where(row == 1, gain_grad_n, 0.0))
    gains_ref[...] = gains.astype(BF16)
    x, core = place_ref[0], place_ref[1]
    moves, coarse_moves = [], []
    for half, offsets in ((0, (0, 1, 3, 2)), (1, (0, 3, 1, 2))):
        for at, offset in enumerate(offsets):
            sides = (keep_far_hbm, send_far_hbm) if at >= 2 else (keep_near_hbm, send_near_hbm)
            for ref, other in zip(sides, (core, 1 - core)):
                block = (x ^ offset) * 2 + other
                unit = ref.at[half, at % 2]
                rows = pl.ds(pl.multiple_of(block * 448 + half * 224, 32), 224)
                moves.append((big_ref.at[rows], unit.at[0:224]))
                moves.append((gains_ref, unit.at[288:304]))
                rows = pl.ds(pl.multiple_of(block * 128 + half * 64, 64), 64)
                coarse_moves.append((coarse_ref.at[rows], unit.at[224:288]))
    weights_left = fetch(moves, move_sems)
    send_grad = dot(back, w_ein_ref[0:512], 1, 1).astype(BF16)
    recv_grad = dot(back, w_ein_ref[512:1024], 1, 1).astype(BF16)
    senders = index_ref[1:2]
    coarse_ref[...] = dot(one_hot_t(senders, 768, 1024), send_grad).astype(BF16)
    coarse_left = fetch(coarse_moves, coarse_sems)
    rim_grad = dot(one_hot_t(index_ref[0:1], 256, 512), send_grad).astype(BF16)
    for at, ref in enumerate((to_core_ref, to_band_ref, to_y_ref, to_sector_ref)):
        ref[...] = rim_grad[128 * at : 128 * at + 128]
    edge_grad_ref[...] = (
        edge_cot + dot(back, w_ein_ref[1024:1536], 1, 1).astype(BF16).astype(F32)
    ).astype(BF16)
    edge_grad_out = pltpu.make_async_copy(edge_grad_ref, edge_grad_hbm, out_sems.at[2])
    edge_grad_out.start()
    own_grad_ref[...] = (
        own_grad
        + dot(one_hot_t(index_ref[2:3], 0, 256), recv_grad)
        + dot(one_hot_t(senders, 0, 256), send_grad)
    )
    own_grad_out = pltpu.make_async_copy(own_grad_ref, own_grad_hbm, out_sems.at[3])
    own_grad_out.start()
    for n in range(len(moves)):
        weights_left(n)
    for n in range(len(coarse_moves)):
        coarse_left(n)
    for copy in (new_edges_out, new_nodes_out, edge_grad_out, own_grad_out):
        copy.wait()


def finish_kernel(
    factor, rim_ref, coarse_ref, own_ref, a_ref, b_ref, c_ref, d_ref, kept_ref, got_ref, out_ref, weights_ref, gains_ref, sum_ref
):
    into = one_hot_t(rim_ref[...], 0, 256)
    total = own_ref[...] + dot(into, a_ref[...]) + dot(into, b_ref[...])
    total = total + dot(into, c_ref[...]) + dot(into, d_ref[...])
    sum_ref[...] = kept_ref[...].astype(F32) + got_ref[...].astype(F32)
    weights_ref[...] = sum_ref[0:14] * factor
    gains_ref[...] = sum_ref[14:16] * factor
    at = lax.broadcasted_iota(jnp.int32, (256, 8), 0)
    coarse_into = (at == coarse_ref[...]).astype(F32)
    total = total + lax.dot_general(
        coarse_into,
        sum_ref[16:24],
        (((1,), (0,)), ((), ())),
        precision=lax.Precision.HIGHEST,
        preferred_element_type=F32,
    )
    out_ref[...] = total.astype(BF16)


def call(kernel, out, *operands, scratch=(), small=(), there=(), out_there=(), flops=0, limit=50):
    def spec(at, away):
        return pl.BlockSpec(memory_space=pltpu.SMEM if at in small else pltpu.HBM if at in away else pltpu.VMEM)

    size = sum(value.size * value.dtype.itemsize for value in operands)
    size += sum(math.prod(shape) * jnp.dtype(dtype).itemsize for shape, dtype in out)
    return pl.pallas_call(
        kernel,
        out_shape=[jax.ShapeDtypeStruct(*leaf) for leaf in out],
        in_specs=[spec(at, there) for at in range(len(operands))],
        out_specs=[pl.BlockSpec(memory_space=pltpu.HBM if at in out_there else pltpu.VMEM) for at in range(len(out))],
        scratch_shapes=list(scratch),
        compiler_params=pltpu.CompilerParams(vmem_limit_bytes=limit * 1024 * 1024),
        cost_estimate=pl.CostEstimate(flops=flops, bytes_accessed=size, transcendentals=0),
    )(*operands)


def on_device(
    node_latent,
    edge_latent,
    senders,
    receivers,
    edge_live,
    halo_list,
    coarse_list,
    edge_in_w,
    edge_out_w,
    node_in_w,
    node_out_w,
    edge_gain,
    node_gain,
    node_cot,
    edge_cot,
):
    nodes, edges = node_latent[0, 0, 0], edge_latent[0, 0, 0]
    send, recv = senders[0], receivers[0]
    rim_list, coarse_ids = halo_list[0], coarse_list[0]
    x, core, *_ = position()
    outgoing, coarse_own = call(
        outgoing_kernel,
        [((128, WIDTH), BF16), ((8, WIDTH), BF16)],
        rim_list,
        coarse_ids,
        nodes,
        scratch=[pltpu.VMEM((256, WIDTH), BF16), pltpu.SemaphoreType.DMA((1,))],
        there=(2,),
        flops=2 * 136 * 256 * 512,
        limit=16,
    )
    far = jnp.where(send >= 768, 768 + coarse_slot(send - 768), 256 + rim_slot(send - 256))
    slot = jnp.where(send < 256, send, far)
    live_recv = jnp.where(edge_live[0] != 0, recv, -1)
    index = jnp.concatenate([slot, send, recv, live_recv, slot, slot, slot, slot], axis=0)
    rows = doubled(coarse_own, ("y", 1))
    rim_y, rim_sector = exchange(outgoing, "y"), exchange(outgoing, "next sector")
    rim_band = exchange(outgoing, "next band")
    rows = doubled(rows, ("ring", 1))
    rows, outgoing, rim_y, rim_band, rim_sector = lax.optimization_barrier((rows, outgoing, rim_y, rim_band, rim_sector))
    rows = doubled(rows, ("ring", -1))
    rows = doubled(rows, ("ring", 3))
    top, low = doubled(rows[:64], ("x", 1)), doubled(rows[64:], ("x", 3))
    top, low, outgoing = lax.optimization_barrier((top, low, outgoing))
    gathered = [doubled(top, ("x", 3)), doubled(low, ("x", 1))]
    gathered += [exchange(rows, "core") for rows in gathered]
    rims = exchange(outgoing, "core"), rim_band, rim_y, rim_sector
    place = jnp.stack([x, core]).astype(jnp.int32)
    new_nodes, new_edges, edge_grad, own_grad, *sums = call(
        layer_kernel,
        [
            ((256, WIDTH), BF16),
            ((384, WIDTH), BF16),
            ((384, WIDTH), BF16),
            ((256, WIDTH), F32),
            *[((128, WIDTH), BF16)] * 4,
            ((2, 2, UNIT, WIDTH), BF16),
            ((2, 2, UNIT, WIDTH), BF16),
            ((2, 2, UNIT, WIDTH), BF16),
            ((2, 2, UNIT, WIDTH), BF16),
        ],
        place,
        index,
        edges,
        nodes,
        *rims,
        *gathered,
        edge_in_w,
        edge_out_w,
        node_in_w,
        node_out_w,
        edge_gain[None],
        node_gain[None],
        node_cot[0, 0, 0],
        edge_cot[0, 0, 0],
        scratch=[
            pltpu.VMEM((3584, WIDTH), BF16),
            pltpu.VMEM((1024, WIDTH), BF16),
            pltpu.VMEM((384, WIDTH), F32),
            pltpu.VMEM((384, WIDTH), BF16),
            pltpu.VMEM((256, WIDTH), BF16),
            pltpu.VMEM((1536, WIDTH), BF16),
            pltpu.VMEM((512, WIDTH), BF16),
            pltpu.VMEM((1024, WIDTH), BF16),
            pltpu.VMEM((512, WIDTH), BF16),
            pltpu.VMEM((256, WIDTH), BF16),
            pltpu.VMEM((384, WIDTH), BF16),
            pltpu.VMEM((256, WIDTH), BF16),
            pltpu.VMEM((384, WIDTH), BF16),
            pltpu.VMEM((384, WIDTH), BF16),
            pltpu.VMEM((256, WIDTH), F32),
            pltpu.VMEM((1536, WIDTH), BF16),
            pltpu.VMEM((16, WIDTH), BF16),
            pltpu.SemaphoreType.DMA((32,)),
            pltpu.SemaphoreType.DMA((16,)),
            pltpu.SemaphoreType.DMA((16,)),
            pltpu.SemaphoreType.DMA((4,)),
        ],
        small=(0,),
        there=(2, 3, 4, 5, 6, 7, 8, 9, 10, 11, 12, 13, 14, 15, 18, 19),
        out_there=(0, 1, 2, 3, 8, 9, 10, 11),
        flops=2 * 384 * 512 * 10000,
    )
    kept, got, back = reduce_all(sums[:4], *sums[4:])
    devices = lax.axis_size("lat") * lax.axis_size("lon") * lax.axis_size("dp")
    node_grad, weight_share, gain_grad = call(
        functools.partial(finish_kernel, 1.0 / math.sqrt(384 * devices)),
        [((256, WIDTH), BF16), ((14, WIDTH), F32), ((2, WIDTH), F32)],
        rim_list,
        coarse_ids,
        own_grad,
        *back,
        kept,
        got,
        scratch=[pltpu.VMEM((24, WIDTH), F32)],
        flops=2 * 512 * 256 * 512,
        limit=16,
    )
    wrap = (None, None, None)
    return (
        new_nodes[wrap],
        new_edges[wrap],
        node_grad[wrap],
        edge_grad[wrap],
        weight_share.reshape(-1),
        gain_grad,
    )


def solution(mesh):
    placed = (
        P("dp", "lat", "lon", None, None),
        P("dp", "lat", "lon", None, None),
        P("lat", "lon", None),
        P("lat", "lon", None),
        P("lat", "lon", None),
        P("lat", "lon", None),
        P("lat", "lon", None),
        P(),
        P(),
        P(),
        P(),
        P(),
        P(),
        P("dp", "lat", "lon", None, None),
        P("dp", "lat", "lon", None, None),
    )
    return jax.shard_map(
        on_device,
        mesh=mesh,
        in_specs=placed,
        out_specs=(
            P("dp", "lat", "lon", None, None),
            P("dp", "lat", "lon", None, None),
            P("dp", "lat", "lon", None, None),
            P("dp", "lat", "lon", None, None),
            P(("lat", "lon", "dp")),
            P(),
        ),
        check_vma=False,
    )
```
